256 devices in a mesh: xy: 64 (over y_lo, x, z), gz: 4 (over y_hi, core).
Axes of the slice: x: 4, y: 4 (y_hi: 2, y_lo: 2; y = y_hi * 2 + y_lo), z: 8, core: 2. Of those that a mesh axis runs over, the one named last changes fastest.
Arguments:
- velocity: float32 [3, 256, 128, 512], P(None, 'xy', 'gz'), may hold values from -6 to 6
- pressure: float32 [256, 128, 512], P('xy', 'gz'), may hold values from -6 to 6
- momentum_source: float32 [3, 256, 128, 512], P(None, 'xy', 'gz'), may hold values from -6 to 6
- continuity_source: float32 [256, 128, 512], P('xy', 'gz'), may hold values from -6 to 6
- reaction: float32 [256, 128, 512], P('xy', 'gz'), may hold values from 0.01 to 0.2
- pressure_weight: float32 [256, 512], P('xy'), may hold values from 0.5 to 2
- mz_inverse: float32 [128, 128], replicated, as said below
Outputs:
- velocity_update: float32 [3, 256, 128, 512], P(None, 'xy', 'gz')
- correction: float32 [256, 128, 512], P('xy', 'gz')
The draws below stay inside these ranges and needn't reach their ends.
Inputs may be any that keep to these rules, and one draw needn't show every extreme that they name: mz_inverse is a full 128 x 128 matrix.
All inputs are finite; a program needn't handle non-finite values.
Results may differ from the reference program's by a relative error of at most 0.00007.
Values sent between devices are 32-bit elements; how exact they have to be, the bound alone decides.
A program may use at most 64 MiB of HBM per device.

```python
import math
import jax
import jax.numpy as jnp
from jax import lax

NY = 512
NX = 256
NZ = 128


def draw_mz_inverse(key, part):
    key = jax.random.fold_in(key, 7)
    diag_key = jax.random.fold_in(key, 1)
    off_key = jax.random.fold_in(key, 2)
    diagonal = jax.random.uniform(diag_key, (NZ,), jnp.float32, 1.0, 3.0)
    off_diagonal = jnp.clip(jax.random.normal(off_key, (NZ, NZ), jnp.float32), -4.0, 4.0) * (0.5 / math.sqrt(NZ))
    matrix = off_diagonal + jnp.eye(NZ, dtype=jnp.float32) * diagonal[:, None]
    return matrix.astype(jnp.float32)


def steps_of(key, extent, cuts, smallest, top_value):
    gain = 1.0
    for axis_at, shards_of in cuts:
        steps = jax.random.uniform(jax.random.fold_in(jax.random.fold_in(key, 6), axis_at), (shards_of,), jnp.float32, smallest / len(cuts), top_value / len(cuts))
        gain = gain * jnp.repeat(jnp.exp(steps), extent[axis_at] // shards_of).reshape((-1,) + (1,) * (len(extent) - 1 - axis_at))
    return gain


def noise(stream_key, dims, scale, most, split=(), kind=jnp.bfloat16):
    entries = jax.random.normal(stream_key, dims, jnp.float32) * scale
    if len(split) > 0:
        entries = steps_of(stream_key, dims, split, -0.22, 0.18) * entries
    return jnp.clip(entries, min=-most, max=most).astype(kind)


def setup_inputs(seed: int = 0) -> dict:
    key_of = jax.random.split(jax.random.key(seed), 8)
    velocity = noise(key_of[0], (3, NX, NZ, NY), 1.0, 6.0, ((1, 64), (2, 4)), jnp.float32)
    pressure = noise(key_of[1], (NX, NZ, NY), 1.0, 6.0, ((0, 64), (1, 4)), jnp.float32)
    momentum_source = noise(key_of[2], (3, NX, NZ, NY), 1.0, 6.0, ((1, 64), (2, 4)), jnp.float32)
    continuity_source = noise(key_of[3], (NX, NZ, NY), 1.0, 6.0, ((0, 64), (1, 4)), jnp.float32)
    reaction = jnp.clip(jnp.exp(math.log(0.2) - 2.9957323 * jax.random.uniform(key_of[4], (NX, NZ, NY), jnp.float32) ** steps_of(key_of[4], (NX, NZ, NY), ((0, 64), (1, 4)), -0.2, 0.2)), 0.01, 0.2)
    pressure_weight = jnp.clip(jnp.exp(math.log(2.0) - 1.3862944 * jax.random.uniform(key_of[5], (NX, NY), jnp.float32) ** steps_of(key_of[5], (NX, NY), ((0, 64),), -0.2, 0.2)), 0.5, 2.0)
    mz_inverse = draw_mz_inverse(jax.random.fold_in(key_of[7], 71), 0)
    return dict(velocity=velocity, pressure=pressure, momentum_source=momentum_source, continuity_source=continuity_source, reaction=reaction, pressure_weight=pressure_weight, mz_inverse=mz_inverse)


MASS_TAPS = (1.0 / 5040.0, 1.0 / 42.0, 397.0 / 1680.0, 151.0 / 315.0, 397.0 / 1680.0, 1.0 / 42.0, 1.0 / 5040.0)
STIFF_TAPS = (-1.0 / 120.0, -0.2, -0.125, 2.0 / 3.0, -0.125, -0.2, -1.0 / 120.0)
DAMPING = 0.5
CENTRE_DIAG = 3.0 * (2.0 / 3.0) * (151.0 / 315.0) ** 2


def apply_band(values, weights, direction):
    length = values.shape[direction] - 6
    summed = weights[0] * lax.slice_in_dim(values, 0, length, axis=direction)
    for offset in range(1, 7):
        summed = summed + weights[offset] * lax.slice_in_dim(values, offset, offset + length, axis=direction)
    return summed


def widen_last(values):
    return jnp.pad(values, ((0, 0), (0, 0), (0, 0), (3, 3)))


def inner_parts(values):
    mass_z = widen_last(apply_band(values, MASS_TAPS, 2))
    stiff_z = widen_last(apply_band(values, STIFF_TAPS, 2))
    outer_mass = apply_band(mass_z, MASS_TAPS, 3)
    outer_stiff = apply_band(mass_z, STIFF_TAPS, 3) + apply_band(stiff_z, MASS_TAPS, 3)
    return outer_mass, outer_stiff


def stiffness(values, reaction):
    padded = jnp.pad(values, ((0, 0), (3, 3), (3, 3), (0, 0)))
    outer_mass, outer_stiff = inner_parts(padded)
    return apply_band(outer_mass, STIFF_TAPS, 1) + apply_band(outer_stiff, MASS_TAPS, 1) + reaction * values


def divergence(values):
    padded = jnp.pad(values, ((0, 0), (0, 1), (0, 1), (0, 1)))
    along_x = padded[0, 1:, :-1, :-1] - values[0]
    along_y = padded[1, :-1, :-1, 1:] - values[1]
    along_z = padded[2, :-1, 1:, :-1] - values[2]
    return along_x + along_y + along_z


def gradient(potential):
    padded = jnp.pad(potential, ((1, 0), (1, 0), (1, 0)))
    along_x = padded[:-1, 1:, 1:] - potential
    along_y = padded[1:, 1:, :-1] - potential
    along_z = padded[1:, :-1, 1:] - potential
    return jnp.stack([along_x, along_y, along_z])


def reference(velocity, pressure, momentum_source, continuity_source, reaction, pressure_weight, mz_inverse):
    applied = stiffness(velocity, reaction)
    pressure_residual = continuity_source - divergence(velocity)
    scaled = -pressure_weight[:, None, :] * pressure_residual
    correction = jnp.einsum("zk,xky->xzy", mz_inverse, scaled, precision=lax.Precision.HIGHEST)
    right_side = momentum_source - applied - gradient(pressure) - gradient(correction)
    diagonal = CENTRE_DIAG + reaction
    first_sweep = DAMPING * right_side / diagonal
    second_sweep = first_sweep + DAMPING * (right_side - stiffness(first_sweep, reaction)) / diagonal
    return second_sweep, correction
```

```python
import functools

import jax
import jax.numpy as jnp
import ml_dtypes
import numpy as np
from jax import lax
from jax.experimental import pallas as pl
from jax.experimental.pallas import tpu as pltpu
from jax.sharding import PartitionSpec as P

MASS_INT = (1.0, 120.0, 1191.0, 2416.0, 1191.0, 120.0, 1.0)
STIFF_INT = (-1.0, -24.0, -15.0, 80.0, -15.0, -24.0, -1.0)
MASS_SCALE = 5040.0
STIFF_SCALE = 120.0
DAMPING = 0.5
CENTRE_DIAG = 3.0 * (2.0 / 3.0) * (151.0 / 315.0) ** 2

PX = 4
PZ = 32
ROWS = PX * PZ
NY = 512
HALO = 3 * PZ
EDGE = 80
DEPTH = ROWS + 2 * HALO + EDGE
MESH = pl.DeviceIdType.MESH
F32 = jnp.float32
BF16 = jnp.bfloat16


def split_np(matrix):
    high = matrix.astype(ml_dtypes.bfloat16)
    low = (matrix - high.astype(np.float64)).astype(ml_dtypes.bfloat16)
    return high, low


def source_points():
    points = [(p, z) for p in range(PX) for z in range(PZ)]
    points += [(p, z) for p in (-3, -2, -1) for z in range(PZ)]
    points += [(p, z) for p in (4, 5, 6) for z in range(PZ)]
    inner, outer = tuple(range(PX)), (-3, -2, -1, 4, 5, 6)
    for planes in (inner, outer):
        for first in (-4, PZ):
            points += [(p, first + j) for p in planes for j in range(4)]
    return points


def operators():
    mass = {o: w / MASS_SCALE for o, w in zip(range(-3, 4), MASS_INT)}
    stiff = {o: w / STIFF_SCALE for o, w in zip(range(-3, 4), STIFF_INT)}
    plane = np.zeros((2 * ROWS, DEPTH), np.float64)
    for column, (x_in, z_in) in enumerate(source_points()):
        for x_out in range(PX):
            for z_out in range(PZ):
                ox, oz = x_in - x_out, z_in - z_out
                if abs(ox) <= 3 and abs(oz) <= 3:
                    row = x_out * PZ + z_out
                    plane[row, column] = (mass[ox] * stiff[oz] + stiff[ox] * mass[oz]) / MASS_SCALE
                    plane[ROWS + row, column] = mass[ox] * mass[oz] / STIFF_SCALE
    mass_y = np.zeros((NY, NY), np.float64)
    stiff_y = np.zeros((NY, NY), np.float64)
    for offset in range(-3, 4):
        mass_y += np.diag(np.full(NY - abs(offset), MASS_INT[offset + 3]), -offset)
        stiff_y += np.diag(np.full(NY - abs(offset), STIFF_INT[offset + 3]), -offset)
    return split_np(plane) + split_np(mass_y) + split_np(stiff_y)[:1]


def split(values):
    high = values.astype(BF16)
    return high, (values - high.astype(F32)).astype(BF16)


def dot(left, right):
    return jnp.dot(left, right, preferred_element_type=F32)


def kernel(
    count_x,
    vel, prs, mom, con, rea, pwt, mzi, sh_a, sl_a, mh_a, ml_a, ky_a,
    out, cor,
    V, PR, MS, CS, RE, PW, MZ, SH, SL, MH, ML, KY,
    XL, XR, ZB, PK, SG, QH, PD, PP, Q, CO, H, BASE, FS, OB, BH, BL, SBH, SBL, QL,
    local_sem, out_sem, send_sem, recv_sem,
):
    i = lax.axis_index("xy")
    g = lax.axis_index("gz")
    left = (lax.rem(i + count_x - 1, count_x), g)
    right = (lax.rem(i + 1, count_x), g)
    upper = (i, lax.rem(g + 1, 4))
    lower = (i, lax.rem(g + 3, 4))
    across = (i, lax.rem(g + 2, 4))
    core = (i, g + 1 - 2 * lax.rem(g, 2))
    has_left, has_right = i > 0, i < count_x - 1
    has_lower, has_upper = g > 0, g < 3

    loads = []

    def load(src, dst):
        copy = pltpu.make_async_copy(src, dst, local_sem.at[len(loads)])
        copy.start()
        loads.append(copy)
        return copy

    load_v = {c: load(vel.at[c], V.at[c]) for c in (2, 0, 1)}
    load_p = load(prs, PR)
    load_c = load(con, CS)
    load_w = load(pwt, PW)
    load_z = load(mzi.at[pl.ds(pl.multiple_of(g * PZ, PZ), PZ)], MZ.at[pl.ds(8, PZ)])
    load_r = load(rea, RE)
    load_ops = [load(a, b) for a, b in ((sh_a, SH), (sl_a, SL), (mh_a, MH), (ml_a, ML), (ky_a, KY))]
    load_m = load(mom, MS)
    above = pl.multiple_of(jnp.maximum(g * PZ - 8, 0), 8)
    load_z2 = pltpu.make_async_copy(mzi.at[pl.ds(above, 8)], MZ.at[pl.ds(0, 8)], local_sem.at[len(loads)])

    @pl.when(has_lower)
    def _():
        load_z2.start()

    @pl.when(jnp.logical_not(has_left))
    def _():
        XL[...] = jnp.zeros_like(XL)
        QH[...] = jnp.zeros_like(QH)

    @pl.when(jnp.logical_not(has_right))
    def _():
        XR[...] = jnp.zeros_like(XR)

    @pl.when(jnp.logical_not(has_lower))
    def _():
        MZ[0:8, :] = jnp.zeros((8, 128), F32)
        PD[...] = jnp.zeros_like(PD)
        for s in range(2):
            for c in range(3):
                ZB[s, c, 0:16, :] = jnp.zeros((16, NY), F32)
                ZB[s, c, 32:56, :] = jnp.zeros((24, NY), F32)

    @pl.when(jnp.logical_not(has_upper))
    def _():
        for s in range(2):
            for c in range(3):
                ZB[s, c, 16:32, :] = jnp.zeros((16, NY), F32)
                ZB[s, c, 56:80, :] = jnp.zeros((24, NY), F32)

    used = [0]

    def remote(src, dst, device, sends, receives):
        at = used[0]
        used[0] += 1
        copy = pltpu.make_async_remote_copy(
            src_ref=src, dst_ref=dst, send_sem=send_sem.at[at], recv_sem=recv_sem.at[at],
            device_id=device, device_id_type=MESH,
        )
        return copy, sends, receives

    started = []

    def start(*copies):
        condition = copies[0][1]
        started.extend(copies)
        if condition is None:
            for copy in copies:
                copy[0].start()
        else:

            @pl.when(condition)
            def _():
                for copy in copies:
                    copy[0].start()

    def arrive(*copies):
        condition = copies[0][2]
        if condition is None:
            for copy in copies:
                copy[0].wait_recv()
        else:

            @pl.when(condition)
            def _():
                for copy in copies:
                    copy[0].wait_recv()

    def to_left(src, dst):
        return remote(src, dst, left, has_left, has_right)

    def to_right(src, dst):
        return remote(src, dst, right, has_right, has_left)

    def to_upper(src, dst):
        return remote(src, dst, upper, has_upper, has_lower)

    def to_lower(src, dst):
        return remote(src, dst, lower, has_lower, has_upper)

    barrier = pltpu.get_barrier_semaphore()
    for device in (left, right, upper, lower, across):
        pl.semaphore_signal(barrier, inc=1, device_id=device, device_id_type=MESH)
    pl.semaphore_wait(barrier, 5)

    v_left = {c: to_left(vel.at[c, pl.ds(0, HALO)], XR.at[0, c]) for c in (1, 2)}
    v_first = to_left(vel.at[0, pl.ds(0, PZ)], XR.at[0, 0, pl.ds(0, PZ)])
    v_left[0] = to_left(vel.at[0, pl.ds(PZ, 2 * PZ)], XR.at[0, 0, pl.ds(PZ, 2 * PZ)])
    v_right = {c: to_right(vel.at[c, pl.ds(PZ, HALO)], XL.at[0, c]) for c in range(3)}
    start(v_first, v_left[1], v_left[2], v_left[0])
    start(v_right[1], v_right[2], v_right[0])

    def edges(s, c, ref):
        for p in range(PX):
            PK[s, c, pl.ds(4 * p, 4), :] = ref[c, pl.ds(p * PZ + PZ - 4, 4), :]
            PK[s, c, pl.ds(16 + 4 * p, 4), :] = ref[c, pl.ds(p * PZ, 4), :]
        down = to_lower(PK.at[s, c, pl.ds(16, 16)], ZB.at[s, c, pl.ds(16, 16)])
        up = to_upper(PK.at[s, c, pl.ds(0, 16)], ZB.at[s, c, pl.ds(0, 16)])
        start(down)
        start(up)
        return down, up

    def corners(s, c):
        for half, ref in enumerate((XL, XR)):
            for p in range(3):
                at = 12 * half + 4 * p
                PK[s, c, pl.ds(32 + at, 4), :] = ref[s, c, pl.ds(p * PZ + PZ - 4, 4), :]
                PK[s, c, pl.ds(56 + at, 4), :] = ref[s, c, pl.ds(p * PZ, 4), :]
        down = to_lower(PK.at[s, c, pl.ds(56, 24)], ZB.at[s, c, pl.ds(56, 24)])
        up = to_upper(PK.at[s, c, pl.ds(32, 24)], ZB.at[s, c, pl.ds(32, 24)])
        start(down)
        start(up)
        return down, up

    edge, corner = {}, {}
    load_v[2].wait()
    edge[0, 2] = edges(0, 2, V)
    load_p.wait()
    for p in range(PX):
        PP[pl.ds(p, 1), :] = PR[pl.ds(p * PZ + PZ - 1, 1), :]
    PP[pl.ds(4, 4), :] = jnp.zeros((4, NY), F32)
    p_rows = to_upper(PP, PD)
    start(p_rows)
    load_v[0].wait()
    load_v[1].wait()
    edge[0, 1] = edges(0, 1, V)
    edge[0, 0] = edges(0, 0, V)

    row_at = lax.broadcasted_iota(jnp.int32, (PZ, NY), 0)
    lane_at = lax.broadcasted_iota(jnp.int32, (PZ, NY), 1)

    def plane(p):
        return pl.ds(p * PZ, PZ)

    mine = pl.ds(pl.multiple_of(g * PZ, PZ), PZ)
    theirs = pl.ds(pl.multiple_of(lax.rem(g + 2, 4) * PZ, PZ), PZ)
    s_across = [remote(SG.at[p, mine], SG.at[p, mine], across, None, None) for p in range(PX)]
    s_core = [remote(SG.at[p, mine], SG.at[p, mine], core, None, None) for p in range(PX)]
    s_next = [remote(SG.at[p, theirs], SG.at[p, theirs], core, None, None) for p in range(PX)]

    def residual(p):
        vx, vy, vz = (V[c, plane(p), :] for c in range(3))
        next_x = XR[0, 0, pl.ds(0, PZ), :] if p == PX - 1 else V[0, plane(p + 1), :]
        next_y = jnp.where(lane_at == NY - 1, 0.0, pltpu.roll(vy, NY - 1, 1))
        beyond = ZB[0, 2, pl.ds(16 + 4 * p, 1), :]
        next_z = jnp.where(row_at == PZ - 1, beyond, pltpu.roll(vz, PZ - 1, 0))
        diverged = (next_x - vx) + (next_y - vy) + (next_z - vz)
        SG[p, mine, :] = -PW[pl.ds(p, 1), :] * (CS[plane(p), :] - diverged)
        start(s_across[p], s_core[p])

    load_c.wait()
    load_w.wait()
    arrive(edge[0, 2][0])
    for p in range(PX - 1):
        residual(p)
    arrive(v_first)
    residual(PX - 1)

    load_r.wait()
    H[...] = DAMPING / (CENTRE_DIAG + RE[...])
    for copy in load_ops:
        copy.wait()
    load_m.wait()
    load_z.wait()

    @pl.when(has_lower)
    def _():
        load_z2.wait()

    def operate(s, c, ref):
        BH[0:ROWS, :], BL[0:ROWS, :] = split(ref[c])
        BH[ROWS:ROWS + HALO, :], BL[ROWS:ROWS + HALO, :] = split(XL[s, c])
        BH[ROWS + HALO:ROWS + 2 * HALO, :], BL[ROWS + HALO:ROWS + 2 * HALO, :] = split(XR[s, c])
        BH[ROWS + 2 * HALO:, :], BL[ROWS + 2 * HALO:, :] = split(ZB[s, c])
        both = dot(SH[...], BH[...]) + (dot(SL[...], BH[...]) + dot(SH[...], BL[...]))
        first_h, first_l = split(both[:ROWS])
        second_h, second_l = split(both[ROWS:])
        mass, stiff = MH[...], KY[...]
        return (dot(first_h, mass) + dot(second_h, stiff)) + (
            dot(first_l, mass) + dot(second_l, stiff) + dot(first_h, ML[...])
        )

    def base(c):
        BASE[c] = MS[c] - operate(0, c, V) - RE[...] * V[c]

    mz_h, mz_l = split(MZ[...])

    def solve(p):
        s_h, s_l = split(SG[p])
        solved = dot(mz_h, s_h) + (dot(mz_l, s_h) + dot(mz_h, s_l))
        CO[plane(p), :] = solved[8:]
        Q[plane(p), :] = solved[8:] + PR[plane(p), :]
        QL[pl.ds(p, 1), :] = solved[7:8] + PD[pl.ds(p, 1), :]

    arrive(v_left[1])
    arrive(v_right[1])
    corner[0, 1] = corners(0, 1)
    for p in range(PX):
        arrive(s_across[p])
        start(s_next[p])
        if p == 2:
            arrive(edge[0, 1][0], corner[0, 1][0])
            arrive(edge[0, 1][1], corner[0, 1][1])
            base(1)
    arrive(v_left[2])
    arrive(v_right[2])
    corner[0, 2] = corners(0, 2)
    arrive(p_rows)
    for p in range(PX):
        arrive(s_core[p], s_next[p])
        solve(p)
    q_plane = to_right(Q.at[plane(PX - 1)], QH)
    start(q_plane)
    c_out = pltpu.make_async_copy(CO, cor, out_sem.at[3])
    c_out.start()

    f_left, f_right = {}, {}

    def sweep(c):
        for p in range(PX):
            q = Q[plane(p), :]
            if c == 0:
                before = QH[...] if p == 0 else Q[plane(p - 1), :]
            elif c == 1:
                before = jnp.where(lane_at == 0, 0.0, pltpu.roll(q, 1, 1))
            else:
                before = jnp.where(row_at == 0, QL[pl.ds(p, 1), :], pltpu.roll(q, 1, 0))
            FS[c, plane(p), :] = H[plane(p), :] * (BASE[c, plane(p), :] - (before - q))
        f_left[c] = to_left(FS.at[c, pl.ds(0, HALO)], XR.at[1, c])
        f_right[c] = to_right(FS.at[c, pl.ds(PZ, HALO)], XL.at[1, c])
        start(f_left[c])
        start(f_right[c])
        edge[1, c] = edges(1, c, FS)

    sweep(1)
    arrive(edge[0, 2][1], corner[0, 2][1])
    arrive(corner[0, 2][0])
    base(2)
    sweep(2)
    arrive(v_left[0])
    arrive(v_right[0])
    corner[0, 0] = corners(0, 0)
    arrive(edge[0, 0][0], corner[0, 0][0])
    arrive(edge[0, 0][1], corner[0, 0][1])
    base(0)
    arrive(q_plane)
    sweep(0)

    outs = []
    for c in (1, 2, 0):
        arrive(f_left[c])
        arrive(f_right[c])
        corner[1, c] = corners(1, c)
        arrive(edge[1, c][0], corner[1, c][0])
        arrive(edge[1, c][1], corner[1, c][1])
        OB[c] = FS[c] * (2.0 - RE[...] * H[...]) - H[...] * operate(1, c, FS)
        copy = pltpu.make_async_copy(OB.at[c], out.at[c], out_sem.at[c])
        copy.start()
        outs.append(copy)

    for copy, sends, _ in started:
        if sends is None:
            copy.wait_send()
        else:
            pl.when(sends)(copy.wait_send)
    c_out.wait()
    for copy in outs:
        copy.wait()


def shards(count_x, velocity, pressure, momentum, continuity, reaction, weight, mz_inverse):
    consts = [jnp.asarray(m) for m in operators()]
    any_spec = pl.BlockSpec(memory_space=pl.ANY)
    f32 = lambda *shape: pltpu.VMEM(shape, F32)
    b16 = lambda *shape: pltpu.VMEM(shape, BF16)
    flat = (ROWS, NY)
    scratch = [
        f32(3, *flat), f32(*flat), f32(3, *flat), f32(*flat), f32(*flat), f32(PX, NY), f32(40, 128),
        b16(2 * ROWS, DEPTH), b16(2 * ROWS, DEPTH), b16(NY, NY), b16(NY, NY), b16(NY, NY),
        f32(2, 3, HALO, NY), f32(2, 3, HALO, NY), f32(2, 3, EDGE, NY), f32(2, 3, EDGE, NY),
        f32(PX, 4 * PZ, NY), f32(PZ, NY), f32(8, NY), f32(8, NY),
        f32(*flat), f32(*flat), f32(*flat), f32(3, *flat), f32(3, *flat), f32(3, *flat),
        b16(DEPTH, NY), b16(DEPTH, NY), b16(16, NY), b16(16, NY), f32(8, NY),
        pltpu.SemaphoreType.DMA((16,)), pltpu.SemaphoreType.DMA((4,)),
        pltpu.SemaphoreType.DMA((64,)), pltpu.SemaphoreType.DMA((64,)),
    ]
    out, cor = pl.pallas_call(
        functools.partial(kernel, count_x),
        name="stokes",
        out_shape=[jax.ShapeDtypeStruct((3, *flat), F32), jax.ShapeDtypeStruct(flat, F32)],
        in_specs=[any_spec] * 12,
        out_specs=[any_spec] * 2,
        scratch_shapes=scratch,
        compiler_params=pltpu.CompilerParams(
            collective_id=0, has_side_effects=True, vmem_limit_bytes=48 << 20
        ),
    )(
        velocity.reshape(3, *flat), pressure.reshape(flat), momentum.reshape(3, *flat),
        continuity.reshape(flat), reaction.reshape(flat), weight, mz_inverse, *consts,
    )
    return out.reshape(3, PX, PZ, NY), cor.reshape(PX, PZ, NY)


def solution(mesh):
    return jax.shard_map(
        functools.partial(shards, mesh.shape["xy"]),
        mesh=mesh,
        in_specs=(
            P(None, "xy", "gz", None),
            P("xy", "gz", None),
            P(None, "xy", "gz", None),
            P("xy", "gz", None),
            P("xy", "gz", None),
            P("xy", None),
            P(),
        ),
        out_specs=(P(None, "xy", "gz", None), P("xy", "gz", None)),
        check_vma=False,
    )
```

```python
import functools

import jax
import jax.numpy as jnp
import ml_dtypes
import numpy as np
from jax import lax
from jax.experimental import pallas as pl
from jax.experimental.pallas import tpu as pltpu
from jax.sharding import PartitionSpec as P

MASS_INT = (1.0, 120.0, 1191.0, 2416.0, 1191.0, 120.0, 1.0)
STIFF_INT = (-1.0, -24.0, -15.0, 80.0, -15.0, -24.0, -1.0)
MASS_SCALE = 5040.0
STIFF_SCALE = 120.0
DAMPING = 0.5
CENTRE_DIAG = 3.0 * (2.0 / 3.0) * (151.0 / 315.0) ** 2

PX = 4
PZ = 32
ROWS = PX * PZ
NY = 512
HALO = 3 * PZ
EDGE = 80
DEPTH = ROWS + 2 * HALO + EDGE
MESH = pl.DeviceIdType.MESH
F32 = jnp.float32
BF16 = jnp.bfloat16


def split_np(matrix):
    high = matrix.astype(ml_dtypes.bfloat16)
    low = (matrix - high.astype(np.float64)).astype(ml_dtypes.bfloat16)
    return high, low


def source_points():
    points = [(p, z) for p in range(PX) for z in range(PZ)]
    points += [(p, z) for p in (-3, -2, -1) for z in range(PZ)]
    points += [(p, z) for p in (4, 5, 6) for z in range(PZ)]
    inner, outer = tuple(range(PX)), (-3, -2, -1, 4, 5, 6)
    for planes in (inner, outer):
        for first in (-4, PZ):
            points += [(p, first + j) for p in planes for j in range(4)]
    return points


def operators():
    mass = {o: w / MASS_SCALE for o, w in zip(range(-3, 4), MASS_INT)}
    stiff = {o: w / STIFF_SCALE for o, w in zip(range(-3, 4), STIFF_INT)}
    plane = np.zeros((2 * ROWS, DEPTH), np.float64)
    for column, (x_in, z_in) in enumerate(source_points()):
        for x_out in range(PX):
            for z_out in range(PZ):
                ox, oz = x_in - x_out, z_in - z_out
                if abs(ox) <= 3 and abs(oz) <= 3:
                    row = x_out * PZ + z_out
                    plane[row, column] = (mass[ox] * stiff[oz] + stiff[ox] * mass[oz]) / MASS_SCALE
                    plane[ROWS + row, column] = mass[ox] * mass[oz] / STIFF_SCALE
    mass_y = np.zeros((NY, NY), np.float64)
    stiff_y = np.zeros((NY, NY), np.float64)
    for offset in range(-3, 4):
        mass_y += np.diag(np.full(NY - abs(offset), MASS_INT[offset + 3]), -offset)
        stiff_y += np.diag(np.full(NY - abs(offset), STIFF_INT[offset + 3]), -offset)
    return split_np(plane) + split_np(mass_y) + split_np(stiff_y)[:1]


def split(values):
    high = values.astype(BF16)
    return high, (values - high.astype(F32)).astype(BF16)


def dot(left, right):
    return jnp.dot(left, right, preferred_element_type=F32)


def kernel(
    count_x,
    vel, prs, mom, con, rea, pwt, mzi, sh_a, sl_a, mh_a, ml_a, ky_a,
    out, cor,
    V, PR, MS, CS, RE, PW, MZ, SH, SL, MH, ML, KY,
    XL, XR, ZB, PK, SG, QH, PD, PP, Q, CO, H, BASE, FS, OB, BH, BL, FW, QL,
    local_sem, out_sem, send_sem, recv_sem,
):
    i = lax.axis_index("xy")
    g = lax.axis_index("gz")
    half = count_x // 2
    left = (lax.rem(i + count_x - 1, count_x), g)
    right = (lax.rem(i + 1, count_x), g)
    upper = (i, lax.rem(g + 1, 4))
    lower = (i, lax.rem(g + 3, 4))
    across = (i, lax.rem(g + 2, 4))
    core = (i, g + 1 - 2 * lax.rem(g, 2))
    has_left, has_right = i > 0, i < count_x - 1
    has_lower, has_upper = g > 0, g < 3
    at_low, at_high = i == half - 1, i == half
    at_middle = jnp.logical_or(at_low, at_high)
    elsewhere = jnp.logical_not(at_middle)
    left_direct = jnp.logical_and(has_left, i != half)
    right_direct = jnp.logical_and(has_right, i != half - 1)

    loads = []

    def load(src, dst):
        copy = pltpu.make_async_copy(src, dst, local_sem.at[len(loads)])
        copy.start()
        loads.append(copy)
        return copy

    load_v = {c: load(vel.at[c], V.at[c]) for c in (2, 0, 1)}
    load_p = load(prs, PR)
    load_c = load(con, CS)
    load_w = load(pwt, PW)
    load_z = load(mzi.at[pl.ds(pl.multiple_of(g * PZ, PZ), PZ)], MZ.at[pl.ds(8, PZ)])
    load_r = load(rea, RE)
    load_ops = [load(a, b) for a, b in ((sh_a, SH), (sl_a, SL), (mh_a, MH), (ml_a, ML), (ky_a, KY))]
    load_m = load(mom, MS)
    above = pl.multiple_of(jnp.maximum(g * PZ - 8, 0), 8)
    load_z2 = pltpu.make_async_copy(mzi.at[pl.ds(above, 8)], MZ.at[pl.ds(0, 8)], local_sem.at[len(loads)])

    barrier = pltpu.get_barrier_semaphore()
    for device in (upper, lower, across):
        pl.semaphore_signal(barrier, inc=1, device_id=device, device_id_type=MESH)

    def greet(condition, *devices):
        @pl.when(condition)
        def _():
            for device in devices:
                pl.semaphore_signal(barrier, inc=1, device_id=device, device_id_type=MESH)

        return len(devices) * condition.astype(jnp.int32)

    greeted = greet(has_left, left) + greet(has_right, right)
    greeted += greet(at_middle, (0, g), (count_x - 1, g))
    greeted += greet(i == 0, (half - 1, g), (half, g))
    greeted += greet(i == count_x - 1, (half - 1, g), (half, g))

    @pl.when(has_lower)
    def _():
        load_z2.start()

    @pl.when(jnp.logical_not(has_left))
    def _():
        XL[...] = jnp.zeros_like(XL)
        QH[...] = jnp.zeros_like(QH)

    @pl.when(jnp.logical_not(has_right))
    def _():
        XR[...] = jnp.zeros_like(XR)

    @pl.when(jnp.logical_not(has_lower))
    def _():
        MZ[0:8, :] = jnp.zeros((8, 128), F32)
        PD[...] = jnp.zeros_like(PD)
        for s in range(2):
            for c in range(3):
                ZB[s, c, 0:16, :] = jnp.zeros((16, NY), F32)
                ZB[s, c, 32:56, :] = jnp.zeros((24, NY), F32)

    @pl.when(jnp.logical_not(has_upper))
    def _():
        for s in range(2):
            for c in range(3):
                ZB[s, c, 16:32, :] = jnp.zeros((16, NY), F32)
                ZB[s, c, 56:80, :] = jnp.zeros((24, NY), F32)

    used = [0]
    started = []

    def remote(src, dst, device, sends, receives, counts=None):
        at = used[0]
        used[0] += 1
        copy = pltpu.make_async_remote_copy(
            src_ref=src, dst_ref=dst, send_sem=send_sem.at[at],
            recv_sem=recv_sem.at[at if counts is None else counts[3]],
            device_id=device, device_id_type=MESH,
        )
        started.append((copy, sends))
        return copy, sends, receives, at

    def guarded(condition, actions):
        if condition is None:
            for action in actions:
                action()
        else:

            @pl.when(condition)
            def _():
                for action in actions:
                    action()

    def start(*copies):
        guarded(copies[0][1], [copy[0].start for copy in copies])

    def arrive(*copies):
        guarded(copies[0][2], [copy[0].wait_recv for copy in copies])

    def to_left(src, dst, direct=True):
        return remote(src, dst, left, has_left if direct else left_direct, has_right)

    def to_right(src, dst, direct=True):
        return remote(src, dst, right, has_right if direct else right_direct, has_left)

    def to_upper(src, dst):
        return remote(src, dst, upper, has_upper, has_lower)

    def to_lower(src, dst):
        return remote(src, dst, lower, has_lower, has_upper)

    def both_ways(s, c, ref, first=0, rows=pl.ds(0, PZ)):
        lefts = (ref.at[c, pl.ds(first, 3 - first), rows], XR.at[s, c, pl.ds(first, 3 - first), rows])
        rights = (ref.at[c, pl.ds(1, 3), rows], XL.at[s, c, :, rows])
        return to_left(*lefts), to_right(*rights)

    def start_late(pair):
        pl.when(left_direct)(pair[0][0].start)
        pl.when(right_direct)(pair[1][0].start)

        def later():
            pl.when(at_high)(pair[0][0].start)
            pl.when(at_low)(pair[1][0].start)

        return later

    def by_planes(s, c, ref):
        pairs, hand_on = [], []
        for p in range(3):
            slot = FW.at[s, p]
            source_l, target_l = ref.at[c, p], XR.at[s, c, p]
            source_r, target_r = ref.at[c, p + 1], XL.at[s, c, p]
            go_l, go_r = to_left(source_l, target_l, False), to_right(source_r, target_r, False)
            out_l = remote(source_l, slot, (0, g), at_high, i == 0)
            out_r = remote(source_r, slot, (count_x - 1, g), at_low, i == count_x - 1)
            on_l = remote(slot, target_l, (half - 1, g), i == 0, None, go_l)
            on_r = remote(slot, target_r, (half, g), i == count_x - 1, None, go_r)
            pairs += [go_l, go_r]
            for copy in (go_l, go_r, out_l, out_r):
                start(copy)
            hand_on.append(((out_l, on_l), (out_r, on_r)))

        def pass_on(p):
            for arriving, leaving in hand_on[p]:
                guarded(leaving[1], [arriving[0].wait_recv, leaving[0].start])

        return pairs, pass_on

    pl.semaphore_wait(barrier, 3 + greeted)

    v_first = to_left(vel.at[0, 0], XR.at[0, 0, 0])
    start(v_first)
    v_halo = {}
    v_halo[1], v_pass = by_planes(0, 1, vel)
    v_halo[2] = both_ways(0, 2, vel)
    v2_later = start_late(v_halo[2])
    v_halo[0] = both_ways(0, 0, vel, 1)
    v0_later = start_late(v_halo[0])

    def edges(s, c, ref):
        for p in range(PX):
            PK[s, c, pl.ds(4 * p, 4), :] = ref[c, p, pl.ds(PZ - 4, 4), :]
            PK[s, c, pl.ds(16 + 4 * p, 4), :] = ref[c, p, pl.ds(0, 4), :]
        down = to_lower(PK.at[s, c, pl.ds(16, 16)], ZB.at[s, c, pl.ds(16, 16)])
        up = to_upper(PK.at[s, c, pl.ds(0, 16)], ZB.at[s, c, pl.ds(0, 16)])
        start(down)
        start(up)
        return down, up

    def corners(s, c):
        down = to_lower(PK.at[s, c, pl.ds(56, 24)], ZB.at[s, c, pl.ds(56, 24)])
        up = to_upper(PK.at[s, c, pl.ds(32, 24)], ZB.at[s, c, pl.ds(32, 24)])

        def send(halo):
            for copy in halo:
                arrive(copy)
            for side, ref in enumerate((XL, XR)):
                for p in range(3):
                    at = 12 * side + 4 * p
                    PK[s, c, pl.ds(32 + at, 4), :] = ref[s, c, p, pl.ds(PZ - 4, 4), :]
                    PK[s, c, pl.ds(56 + at, 4), :] = ref[s, c, p, pl.ds(0, 4), :]
            start(down)
            start(up)

        return (down, up), send

    edge, corner, send_corner = {}, {}, {}
    for s in range(2):
        for c in range(3):
            corner[s, c], send_corner[s, c] = corners(s, c)

    def arrive_z(s, c):
        for j in range(2):
            if (s, c, j) != (0, 2, 0):
                arrive(edge[s, c][j])
            arrive(corner[s, c][j])

    load_v[2].wait()
    edge[0, 2] = edges(0, 2, V)
    load_p.wait()
    for p in range(PX):
        PP[pl.ds(p, 1), :] = PR[p, pl.ds(PZ - 1, 1), :]
    PP[pl.ds(4, 4), :] = jnp.zeros((4, NY), F32)
    p_rows = to_upper(PP, PD)
    start(p_rows)
    load_v[0].wait()
    load_v[1].wait()
    edge[0, 1] = edges(0, 1, V)
    edge[0, 0] = edges(0, 0, V)

    row_at = lax.broadcasted_iota(jnp.int32, (PZ, NY), 0)
    lane_at = lax.broadcasted_iota(jnp.int32, (PZ, NY), 1)

    mine = pl.ds(pl.multiple_of(g * PZ, PZ), PZ)
    theirs = pl.ds(pl.multiple_of(lax.rem(g + 2, 4) * PZ, PZ), PZ)
    s_across = [remote(SG.at[p, mine], SG.at[p, mine], across, None, None) for p in range(PX)]
    s_core = [remote(SG.at[p, mine], SG.at[p, mine], core, None, None) for p in range(PX)]
    s_next = [remote(SG.at[p, theirs], SG.at[p, theirs], core, None, None) for p in range(PX)]

    def residual(p):
        vx, vy, vz = (V[c, p] for c in range(3))
        next_x = XR[0, 0, 0] if p == PX - 1 else V[0, p + 1]
        next_y = jnp.where(lane_at == NY - 1, 0.0, pltpu.roll(vy, NY - 1, 1))
        beyond = ZB[0, 2, pl.ds(16 + 4 * p, 1), :]
        next_z = jnp.where(row_at == PZ - 1, beyond, pltpu.roll(vz, PZ - 1, 0))
        diverged = (next_x - vx) + (next_y - vy) + (next_z - vz)
        SG[p, mine, :] = -PW[pl.ds(p, 1), :] * (CS[p] - diverged)
        start(s_across[p], s_core[p])

    load_c.wait()
    load_w.wait()
    arrive(edge[0, 2][0])
    for p in range(PX - 1):
        residual(p)
    arrive(v_first)
    residual(PX - 1)
    v_pass(0)

    load_r.wait()
    H[...] = DAMPING / (CENTRE_DIAG + RE[...])
    for copy in load_ops:
        copy.wait()
    load_m.wait()
    load_z.wait()

    @pl.when(has_lower)
    def _():
        load_z2.wait()

    def flat(values):
        return values.reshape(-1, NY)

    def operate(s, c, ref):
        BH[0:ROWS, :], BL[0:ROWS, :] = split(flat(ref[c]))
        BH[ROWS:ROWS + HALO, :], BL[ROWS:ROWS + HALO, :] = split(flat(XL[s, c]))
        BH[ROWS + HALO:ROWS + 2 * HALO, :], BL[ROWS + HALO:ROWS + 2 * HALO, :] = split(flat(XR[s, c]))
        BH[ROWS + 2 * HALO:, :], BL[ROWS + 2 * HALO:, :] = split(ZB[s, c])
        both = dot(SH[...], BH[...]) + (dot(SL[...], BH[...]) + dot(SH[...], BL[...]))
        first_h, first_l = split(both[:ROWS])
        second_h, second_l = split(both[ROWS:])
        mass, stiff = MH[...], KY[...]
        return ((dot(first_h, mass) + dot(second_h, stiff)) + (
            dot(first_l, mass) + dot(second_l, stiff) + dot(first_h, ML[...])
        )).reshape(PX, PZ, NY)

    def base(c):
        BASE[c] = MS[c] - operate(0, c, V) - RE[...] * V[c]

    mz_h, mz_l = split(MZ[...])

    def solve(p):
        s_h, s_l = split(SG[p])
        solved = dot(mz_h, s_h) + (dot(mz_l, s_h) + dot(mz_h, s_l))
        CO[p] = solved[8:]
        Q[p] = solved[8:] + PR[p]
        QL[pl.ds(p, 1), :] = solved[7:8] + PD[pl.ds(p, 1), :]

    def sweep(c):
        for p in range(PX):
            q = Q[p]
            if c == 0:
                before = QH[...] if p == 0 else Q[p - 1]
            elif c == 1:
                before = jnp.where(lane_at == 0, 0.0, pltpu.roll(q, 1, 1))
            else:
                before = jnp.where(row_at == 0, QL[pl.ds(p, 1), :], pltpu.roll(q, 1, 0))
            FS[c, p] = H[p] * (BASE[c, p] - (before - q))

    v_pass(1)
    v_pass(2)
    for p in range(2):
        arrive(s_across[p])
        start(s_next[p])
    send_corner[0, 1](v_halo[1])
    for p in range(2, PX):
        arrive(s_across[p])
        start(s_next[p])
    v2_later()
    pl.when(elsewhere)(lambda: send_corner[0, 2](v_halo[2]))
    arrive_z(0, 1)
    base(1)
    arrive(p_rows)
    for p in reversed(range(PX)):
        arrive(s_core[p], s_next[p])
        solve(p)
    q_plane = to_right(Q.at[PX - 1], QH)
    start(q_plane)
    c_out = pltpu.make_async_copy(CO, cor, out_sem.at[3])
    c_out.start()
    f_halo = {}
    sweep(1)
    f_halo[1], f_pass = by_planes(1, 1, FS)
    edge[1, 1] = edges(1, 1, FS)
    pl.when(at_middle)(lambda: send_corner[0, 2](v_halo[2]))
    v0_later()
    arrive_z(0, 2)
    base(2)
    sweep(2)
    f_halo[2] = both_ways(1, 2, FS)
    start(f_halo[2][0])
    start(f_halo[2][1])
    edge[1, 2] = edges(1, 2, FS)
    send_corner[0, 0](v_halo[0])
    f_pass(0)
    arrive_z(0, 0)
    base(0)
    arrive(q_plane)
    sweep(0)
    f_ends = both_ways(1, 0, FS, rows=pl.ds(0, 8)) + both_ways(1, 0, FS, rows=pl.ds(24, 8))
    f_rest = both_ways(1, 0, FS, rows=pl.ds(8, 16))
    for copy in f_ends + f_rest:
        start(copy)
    edge[1, 0] = edges(1, 0, FS)
    f_pass(1)
    f_pass(2)

    outs = []

    def finish(c):
        OB[c] = FS[c] * (2.0 - RE[...] * H[...]) - H[...] * operate(1, c, FS)
        copy = pltpu.make_async_copy(OB.at[c], out.at[c], out_sem.at[c])
        copy.start()
        outs.append(copy)

    send_corner[1, 1](f_halo[1])
    arrive_z(1, 1)
    finish(1)
    send_corner[1, 2](f_halo[2])
    send_corner[1, 0](f_ends)
    arrive_z(1, 2)
    finish(2)
    for copy in f_rest:
        arrive(copy)
    arrive_z(1, 0)
    finish(0)

    for copy, sends in started:
        guarded(sends, [copy.wait_send])
    c_out.wait()
    for copy in outs:
        copy.wait()


def shards(count_x, velocity, pressure, momentum, continuity, reaction, weight, mz_inverse):
    consts = [jnp.asarray(m) for m in operators()]
    any_spec = pl.BlockSpec(memory_space=pl.ANY)
    f32 = lambda *shape: pltpu.VMEM(shape, F32)
    b16 = lambda *shape: pltpu.VMEM(shape, BF16)
    grid = (PX, PZ, NY)
    halo = (2, 3, 3, PZ, NY)
    scratch = [
        f32(3, *grid), f32(*grid), f32(3, *grid), f32(*grid), f32(*grid), f32(PX, NY), f32(40, 128),
        b16(2 * ROWS, DEPTH), b16(2 * ROWS, DEPTH), b16(NY, NY), b16(NY, NY), b16(NY, NY),
        f32(*halo), f32(*halo), f32(2, 3, EDGE, NY), f32(2, 3, EDGE, NY),
        f32(PX, 4 * PZ, NY), f32(PZ, NY), f32(8, NY), f32(8, NY),
        f32(*grid), f32(*grid), f32(*grid), f32(3, *grid), f32(3, *grid), f32(3, *grid),
        b16(DEPTH, NY), b16(DEPTH, NY), f32(2, 3, PZ, NY), f32(8, NY),
        pltpu.SemaphoreType.DMA((16,)), pltpu.SemaphoreType.DMA((4,)),
        pltpu.SemaphoreType.DMA((128,)), pltpu.SemaphoreType.DMA((128,)),
    ]
    return pl.pallas_call(
        functools.partial(kernel, count_x),
        name="stokes",
        out_shape=[jax.ShapeDtypeStruct((3, *grid), F32), jax.ShapeDtypeStruct(grid, F32)],
        in_specs=[pl.BlockSpec(memory_space=pltpu.HBM)] * 12,
        out_specs=[any_spec] * 2,
        scratch_shapes=scratch,
        compiler_params=pltpu.CompilerParams(
            collective_id=0, has_side_effects=True, vmem_limit_bytes=62 << 20
        ),
    )(velocity, pressure, momentum, continuity, reaction, weight, mz_inverse, *consts)


def solution(mesh):
    return jax.shard_map(
        functools.partial(shards, mesh.shape["xy"]),
        mesh=mesh,
        in_specs=(
            P(None, "xy", "gz", None),
            P("xy", "gz", None),
            P(None, "xy", "gz", None),
            P("xy", "gz", None),
            P("xy", "gz", None),
            P("xy", None),
            P(),
        ),
        out_specs=(P(None, "xy", "gz", None), P("xy", "gz", None)),
        check_vma=False,
    )
```

```python
import functools

import jax
import jax.numpy as jnp
import ml_dtypes
import numpy as np
from jax import lax
from jax.experimental import pallas as pl
from jax.experimental.pallas import tpu as pltpu
from jax.sharding import PartitionSpec as P

MASS_INT = (1.0, 120.0, 1191.0, 2416.0, 1191.0, 120.0, 1.0)
STIFF_INT = (-1.0, -24.0, -15.0, 80.0, -15.0, -24.0, -1.0)
MASS_SCALE = 5040.0
STIFF_SCALE = 120.0
DAMPING = 0.5
CENTRE_DIAG = 3.0 * (2.0 / 3.0) * (151.0 / 315.0) ** 2

PX = 4
PZ = 32
ROWS = PX * PZ
NY = 512
HALO = 3 * PZ
EDGE = 80
NEAR = ROWS + 32
FAR = 2 * HALO + 48
MESH = pl.DeviceIdType.MESH
F32 = jnp.float32
BF16 = jnp.bfloat16


def split_np(matrix):
    high = matrix.astype(ml_dtypes.bfloat16)
    low = (matrix - high.astype(np.float64)).astype(ml_dtypes.bfloat16)
    return high, low


def source_points():
    inner, left, right = tuple(range(PX)), (-3, -2, -1), (4, 5, 6)

    def ends(planes):
        return [(p, first + j) for first in (-4, PZ) for p in planes for j in range(4)]

    near = [(p, z) for p in inner for z in range(PZ)] + ends(inner)
    far = [(p, z) for p in left + right for z in range(PZ)] + ends(left + right)
    return near + [None] * (256 - len(near)) + far


def operators():
    mass = {o: w / MASS_SCALE for o, w in zip(range(-3, 4), MASS_INT)}
    stiff = {o: w / STIFF_SCALE for o, w in zip(range(-3, 4), STIFF_INT)}
    points = source_points()
    plane = np.zeros((2 * ROWS, len(points)), np.float64)
    for column, point in enumerate(points):
        if point is None:
            continue
        x_in, z_in = point
        for x_out in range(PX):
            for z_out in range(PZ):
                ox, oz = x_in - x_out, z_in - z_out
                if abs(ox) <= 3 and abs(oz) <= 3:
                    row = x_out * PZ + z_out
                    plane[row, column] = (mass[ox] * stiff[oz] + stiff[ox] * mass[oz]) / MASS_SCALE
                    plane[ROWS + row, column] = mass[ox] * mass[oz] / STIFF_SCALE
    mass_y = np.zeros((NY, NY), np.float64)
    stiff_y = np.zeros((NY, NY), np.float64)
    for offset in range(-3, 4):
        mass_y += np.diag(np.full(NY - abs(offset), MASS_INT[offset + 3]), -offset)
        stiff_y += np.diag(np.full(NY - abs(offset), STIFF_INT[offset + 3]), -offset)
    half = NY // 2

    def halves(matrix):
        low = slice(half // 2, half + half // 2)
        across = matrix[low, low].copy()
        across[:half // 2, :half // 2] = 0
        across[half // 2:, half // 2:] = 0
        return np.stack([matrix[:half, :half], across])

    mass_h, mass_l = split_np(halves(mass_y))
    return split_np(plane) + (mass_h, mass_l, split_np(halves(stiff_y))[0])


def split(values):
    high = values.astype(BF16)
    return high, (values - high.astype(F32)).astype(BF16)


def dot(left, right):
    return jnp.dot(left, right, preferred_element_type=F32)


def kernel(
    count_x,
    vel, prs, mom, con, rea, pwt, mzi, sh_a, sl_a, mh_a, ml_a, ky_a,
    out, cor,
    V, PR, MS, CS, RE, PW, MZ, SH, SL, MH, ML, KY,
    XL, XR, ZB, PK, SG, QH, PD, PP, Q, CO, H, BASE, FS, OB, NH, NL, BH, BL, TE, FW, QL,
    local_sem, out_sem, send_sem, recv_sem,
):
    i = lax.axis_index("xy")
    g = lax.axis_index("gz")
    half = count_x // 2
    left = (lax.rem(i + count_x - 1, count_x), g)
    right = (lax.rem(i + 1, count_x), g)
    upper = (i, lax.rem(g + 1, 4))
    lower = (i, lax.rem(g + 3, 4))
    across = (i, lax.rem(g + 2, 4))
    core = (i, g + 1 - 2 * lax.rem(g, 2))
    has_left, has_right = i > 0, i < count_x - 1
    has_lower, has_upper = g > 0, g < 3
    at_low, at_high = i == half - 1, i == half
    at_middle = jnp.logical_or(at_low, at_high)
    elsewhere = jnp.logical_not(at_middle)
    left_direct = jnp.logical_and(has_left, i != half)
    right_direct = jnp.logical_and(has_right, i != half - 1)
    at_first, at_last = i == 0, i == count_x - 1
    step = 8 if count_x > 16 else 1
    at_low_side, at_high_side = i == step - 1, i == count_x - step

    loads = []

    def load(src, dst):
        copy = pltpu.make_async_copy(src, dst, local_sem.at[len(loads)])
        copy.start()
        loads.append(copy)
        return copy

    load_v = {c: load(vel.at[c], V.at[c]) for c in (2, 0, 1)}
    load_p = load(prs, PR)
    load_c = load(con, CS)
    load_w = load(pwt, PW)
    load_z = load(mzi.at[pl.ds(pl.multiple_of(g * PZ, PZ), PZ)], MZ.at[pl.ds(8, PZ)])
    load_r = load(rea, RE)
    load_ops = [load(a, b) for a, b in ((sh_a, SH), (sl_a, SL), (mh_a, MH), (ml_a, ML), (ky_a, KY))]
    load_m = load(mom, MS)
    above = pl.multiple_of(jnp.maximum(g * PZ - 8, 0), 8)
    load_z2 = pltpu.make_async_copy(mzi.at[pl.ds(above, 8)], MZ.at[pl.ds(0, 8)], local_sem.at[len(loads)])

    barrier = pltpu.get_barrier_semaphore()
    for device in (upper, lower, across):
        pl.semaphore_signal(barrier, inc=1, device_id=device, device_id_type=MESH)

    def greet(condition, *devices):
        @pl.when(condition)
        def _():
            for device in devices:
                pl.semaphore_signal(barrier, inc=1, device_id=device, device_id_type=MESH)

        return len(devices) * condition.astype(jnp.int32)

    greeted = greet(has_left, left) + greet(has_right, right)
    greeted += greet(at_middle, (0, g), (count_x - 1, g), (step - 1, g), (count_x - step, g))
    greeted += greet(at_low_side, (half - 1, g), (half, g))
    greeted += greet(at_high_side, (half - 1, g), (half, g))
    greeted += greet(i == 0, (half - 1, g), (half, g))
    greeted += greet(i == count_x - 1, (half - 1, g), (half, g))

    @pl.when(has_lower)
    def _():
        load_z2.start()

    @pl.when(jnp.logical_not(has_left))
    def _():
        XL[...] = jnp.zeros_like(XL)
        QH[...] = jnp.zeros_like(QH)

    @pl.when(jnp.logical_not(has_right))
    def _():
        XR[...] = jnp.zeros_like(XR)

    @pl.when(jnp.logical_not(has_lower))
    def _():
        MZ[0:8, :] = jnp.zeros((8, 128), F32)
        PD[...] = jnp.zeros_like(PD)
        for s in range(2):
            for c in range(3):
                ZB[s, c, 0:16, :] = jnp.zeros((16, NY), F32)
                ZB[s, c, 32:56, :] = jnp.zeros((24, NY), F32)

    @pl.when(jnp.logical_not(has_upper))
    def _():
        for s in range(2):
            for c in range(3):
                ZB[s, c, 16:32, :] = jnp.zeros((16, NY), F32)
                ZB[s, c, 56:80, :] = jnp.zeros((24, NY), F32)

    used = [0]
    started = []

    def remote(src, dst, device, sends, receives, counts=None):
        at = used[0]
        used[0] += 1
        copy = pltpu.make_async_remote_copy(
            src_ref=src, dst_ref=dst, send_sem=send_sem.at[at],
            recv_sem=recv_sem.at[at if counts is None else counts[3]],
            device_id=device, device_id_type=MESH,
        )
        started.append((copy, sends))
        return copy, sends, receives, at

    def guarded(condition, actions):
        if condition is None:
            for action in actions:
                action()
        else:

            @pl.when(condition)
            def _():
                for action in actions:
                    action()

    def start(*copies):
        guarded(copies[0][1], [copy[0].start for copy in copies])

    def arrive(*copies):
        guarded(copies[0][2], [copy[0].wait_recv for copy in copies])

    def to_left(src, dst, direct=False):
        if direct:
            return remote(src, dst, left, has_left, has_right)
        return remote(src, dst, left, left_direct, right_direct)

    def to_right(src, dst, direct=False):
        if direct:
            return remote(src, dst, right, has_right, has_left)
        return remote(src, dst, right, right_direct, left_direct)

    def to_upper(src, dst):
        return remote(src, dst, upper, has_upper, has_lower)

    def to_lower(src, dst):
        return remote(src, dst, lower, has_lower, has_upper)

    def both_ways(s, c, ref, first=0, rows=pl.ds(0, PZ), direct=False):
        lefts = (ref.at[c, pl.ds(first, 3 - first), rows], XR.at[s, c, pl.ds(first, 3 - first), rows])
        rights = (ref.at[c, pl.ds(1, 3), rows], XL.at[s, c, :, rows])
        pair = to_left(*lefts, direct), to_right(*rights, direct)
        for copy in pair:
            start(copy)
        return pair

    def middle(s, c, ref, turns, first=0, now=True):
        ends = ((0, at_first), (count_x - 1, at_last))
        sides = ((step - 1, at_low_side), (count_x - step, at_high_side))
        hops = []
        for p in range(3):
            by_left, by_right = sides if turns[p] == 2 else (ends[turns[p]], ends[1 - turns[p]])
            slot = FW.at[s, c, p]
            hop = []
            if p >= first:
                out = remote(ref.at[c, p], slot, (by_left[0], g), at_high, by_left[1])
                hop.append((out, remote(slot, XR.at[s, c, p], (half - 1, g), by_left[1], at_low)))
            out = remote(ref.at[c, p + 1], slot, (by_right[0], g), at_low, by_right[1])
            hop.append((out, remote(slot, XL.at[s, c, p], (half, g), by_right[1], at_high)))
            hops.append(hop)

        def pass_on(*planes):
            for p in planes:
                for out, on in hops[p]:
                    guarded(on[1], [out[0].wait_recv, on[0].start])

        def send():
            for hop in hops:
                for out, _ in hop:
                    start(out)

        if now:
            send()
        return tuple(on for hop in hops for _, on in hop), pass_on, send

    pl.semaphore_wait(barrier, 3 + greeted)

    v_first = to_left(vel.at[0, 0], XR.at[0, 0, 0], True)
    start(v_first)
    v_halo, v_pass, f_halo, f_pass = {}, {}, {}, {}
    for c, turns, first in ((1, (2, 2, 2), 0), (2, (1, 1, 1), 0), (0, (0, 0, 0), 1)):
        across_middle, v_pass[c], v_send = middle(0, c, vel, turns, first, c > 0)
        v_halo[c] = both_ways(0, c, vel, first) + across_middle

    def edges(s, c, ref):
        for p in range(PX):
            PK[s, c, pl.ds(4 * p, 4), :] = ref[c, p, pl.ds(PZ - 4, 4), :]
            PK[s, c, pl.ds(16 + 4 * p, 4), :] = ref[c, p, pl.ds(0, 4), :]
        down = to_lower(PK.at[s, c, pl.ds(16, 16)], ZB.at[s, c, pl.ds(16, 16)])
        up = to_upper(PK.at[s, c, pl.ds(0, 16)], ZB.at[s, c, pl.ds(0, 16)])
        start(down)
        start(up)
        return down, up

    def corners(s, c):
        down = to_lower(PK.at[s, c, pl.ds(56, 24)], ZB.at[s, c, pl.ds(56, 24)])
        up = to_upper(PK.at[s, c, pl.ds(32, 24)], ZB.at[s, c, pl.ds(32, 24)])

        def send(halo):
            for copy in halo:
                arrive(copy)
            for side, ref in enumerate((XL, XR)):
                for p in range(3):
                    at = 12 * side + 4 * p
                    PK[s, c, pl.ds(32 + at, 4), :] = ref[s, c, p, pl.ds(PZ - 4, 4), :]
                    PK[s, c, pl.ds(56 + at, 4), :] = ref[s, c, p, pl.ds(0, 4), :]
            start(down)
            start(up)

        return (down, up), send

    edge, corner, send_corner = {}, {}, {}
    for s in range(2):
        for c in range(3):
            corner[s, c], send_corner[s, c] = corners(s, c)

    load_v[2].wait()
    edge[0, 2] = edges(0, 2, V)
    load_p.wait()
    for p in range(PX):
        PP[pl.ds(p, 1), :] = PR[p, pl.ds(PZ - 1, 1), :]
    PP[pl.ds(4, 4), :] = jnp.zeros((4, NY), F32)
    p_rows = to_upper(PP, PD)
    start(p_rows)
    load_v[0].wait()
    load_v[1].wait()
    edge[0, 1] = edges(0, 1, V)
    edge[0, 0] = edges(0, 0, V)

    row_at = lax.broadcasted_iota(jnp.int32, (PZ, NY), 0)
    lane_at = lax.broadcasted_iota(jnp.int32, (PZ, NY), 1)

    mine = pl.ds(pl.multiple_of(g * PZ, PZ), PZ)
    theirs = pl.ds(pl.multiple_of(lax.rem(g + 2, 4) * PZ, PZ), PZ)
    s_across = [remote(SG.at[p, mine], SG.at[p, mine], across, None, None) for p in range(PX)]
    s_core = [remote(SG.at[p, mine], SG.at[p, mine], core, None, None) for p in range(PX)]
    s_next = [remote(SG.at[p, theirs], SG.at[p, theirs], core, None, None) for p in range(PX)]

    def residual(p):
        vx, vy, vz = (V[c, p] for c in range(3))
        next_x = XR[0, 0, 0] if p == PX - 1 else V[0, p + 1]
        next_y = jnp.where(lane_at == NY - 1, 0.0, pltpu.roll(vy, NY - 1, 1))
        beyond = ZB[0, 2, pl.ds(16 + 4 * p, 1), :]
        next_z = jnp.where(row_at == PZ - 1, beyond, pltpu.roll(vz, PZ - 1, 0))
        diverged = (next_x - vx) + (next_y - vy) + (next_z - vz)
        SG[p, mine, :] = -PW[pl.ds(p, 1), :] * (CS[p] - diverged)
        start(s_across[p], s_core[p])

    load_c.wait()
    load_w.wait()
    arrive(edge[0, 2][0])
    for p in range(PX - 1):
        residual(p)
    arrive(v_first)
    residual(PX - 1)
    v_pass[1](0)

    load_r.wait()
    H[...] = DAMPING / (CENTRE_DIAG + RE[...])
    for copy in load_ops:
        copy.wait()
    load_m.wait()
    load_z.wait()

    @pl.when(has_lower)
    def _():
        load_z2.wait()

    def flat(values):
        return values.reshape(-1, NY)

    def plane_part(columns, high, low):
        return dot(SH[:, columns], high) + (dot(SL[:, columns], high) + dot(SH[:, columns], low))

    def near_part(s, c, ref):
        for j in range(2):
            if (s, c, j) != (0, 2, 0):
                arrive(edge[s, c][j])
        NH[0:ROWS, :], NL[0:ROWS, :] = split(flat(ref[c]))
        NH[ROWS:, :], NL[ROWS:, :] = split(ZB[s, c, 0:32])
        TE[c] = plane_part(slice(0, NEAR), NH[...], NL[...])

    def along_y(first, second):
        parts = split(first) + split(second)

        def product(at, cut):
            first_h, first_l, second_h, second_l = (cut(part) for part in parts)
            mass, stiff = MH[at], KY[at]
            return (dot(first_h, mass) + dot(second_h, stiff)) + (
                dot(first_l, mass) + dot(second_l, stiff) + dot(first_h, ML[at])
            )

        main = product(0, lambda a: jnp.concatenate([a[:, :256], a[:, 256:]], axis=0))
        cross = product(1, lambda a: a[:, 128:384])
        return jnp.concatenate(
            [main[:ROWS, :128], main[:ROWS, 128:] + cross[:, :128],
             main[ROWS:, :128] + cross[:, 128:], main[ROWS:, 128:]], axis=1
        )

    def operate(s, c):
        for j in range(2):
            arrive(corner[s, c][j])
        BH[0:HALO, :], BL[0:HALO, :] = split(flat(XL[s, c]))
        BH[HALO:2 * HALO, :], BL[HALO:2 * HALO, :] = split(flat(XR[s, c]))
        BH[2 * HALO:, :], BL[2 * HALO:, :] = split(ZB[s, c, 32:80])
        both = TE[c] + plane_part(slice(256, 256 + FAR), BH[...], BL[...])
        return along_y(both[:ROWS], both[ROWS:]).reshape(PX, PZ, NY)

    def base(c):
        BASE[c] = MS[c] - operate(0, c) - RE[...] * V[c]

    mz_h, mz_l = split(MZ[...])
    near_part(0, 1, V)

    def solve(p):
        s_h, s_l = split(SG[p])
        solved = dot(mz_h, s_h) + (dot(mz_l, s_h) + dot(mz_h, s_l))
        CO[p] = solved[8:]
        Q[p] = solved[8:] + PR[p]
        QL[pl.ds(p, 1), :] = solved[7:8] + PD[pl.ds(p, 1), :]

    def sweep(c):
        for p in range(PX):
            q = Q[p]
            if c == 0:
                before = QH[...] if p == 0 else Q[p - 1]
            elif c == 1:
                before = jnp.where(lane_at == 0, 0.0, pltpu.roll(q, 1, 1))
            else:
                before = jnp.where(row_at == 0, QL[pl.ds(p, 1), :], pltpu.roll(q, 1, 0))
            FS[c, p] = H[p] * (BASE[c, p] - (before - q))

    v_pass[1](1, 2)
    for p in range(2):
        arrive(s_across[p])
        start(s_next[p])
    send_corner[0, 1](v_halo[1])
    near_part(0, 2, V)
    for p in range(2, PX):
        arrive(s_across[p])
        start(s_next[p])
    v_send()
    v_pass[2](0, 1, 2)
    pl.when(elsewhere)(lambda: send_corner[0, 2](v_halo[2]))
    near_part(0, 0, V)
    base(1)
    arrive(p_rows)
    for p in reversed(range(PX)):
        arrive(s_core[p], s_next[p])
        solve(p)
    q_plane = to_right(Q.at[PX - 1], QH, True)
    start(q_plane)
    c_out = pltpu.make_async_copy(CO, cor, out_sem.at[3])
    c_out.start()
    sweep(1)
    across_middle, f_pass[1], _ = middle(1, 1, FS, (2, 2, 2))
    f_halo[1] = both_ways(1, 1, FS) + across_middle
    edge[1, 1] = edges(1, 1, FS)
    v_pass[0](0, 1, 2)
    pl.when(at_middle)(lambda: send_corner[0, 2](v_halo[2]))
    base(2)
    sweep(2)
    across_middle, f_pass[2], _ = middle(1, 2, FS, (2, 2, 2))
    f_halo[2] = both_ways(1, 2, FS) + across_middle
    edge[1, 2] = edges(1, 2, FS)
    send_corner[0, 0](v_halo[0])
    near_part(1, 1, FS)
    base(0)
    arrive(q_plane)
    sweep(0)
    f_ends = sum((both_ways(1, 0, FS, rows=pl.ds(at, 8), direct=True) for at in (0, 24)), ())
    f_rest = both_ways(1, 0, FS, rows=pl.ds(8, 16), direct=True)
    edge[1, 0] = edges(1, 0, FS)
    f_pass[1](0, 1, 2)
    near_part(1, 2, FS)

    outs = []

    def finish(c):
        OB[c] = FS[c] * (2.0 - RE[...] * H[...]) - H[...] * operate(1, c)
        copy = pltpu.make_async_copy(OB.at[c], out.at[c], out_sem.at[c])
        copy.start()
        outs.append(copy)

    send_corner[1, 1](f_halo[1])
    f_pass[2](0, 1, 2)
    near_part(1, 0, FS)
    finish(1)
    send_corner[1, 2](f_halo[2])
    send_corner[1, 0](f_ends)
    finish(2)
    for copy in f_rest:
        arrive(copy)
    finish(0)

    for copy, sends in started:
        guarded(sends, [copy.wait_send])
    c_out.wait()
    for copy in outs:
        copy.wait()


def shards(count_x, velocity, pressure, momentum, continuity, reaction, weight, mz_inverse):
    consts = [jnp.asarray(m) for m in operators()]
    any_spec = pl.BlockSpec(memory_space=pl.ANY)
    f32 = lambda *shape: pltpu.VMEM(shape, F32)
    b16 = lambda *shape: pltpu.VMEM(shape, BF16)
    grid = (PX, PZ, NY)
    halo = (2, 3, 3, PZ, NY)
    scratch = [
        f32(3, *grid), f32(*grid), f32(3, *grid), f32(*grid), f32(*grid), f32(PX, NY), f32(40, 128),
        b16(2 * ROWS, 256 + FAR), b16(2 * ROWS, 256 + FAR), b16(2, 256, 256), b16(2, 256, 256), b16(2, 256, 256),
        f32(*halo), f32(*halo), f32(2, 3, EDGE, NY), f32(2, 3, EDGE, NY),
        f32(PX, 4 * PZ, NY), f32(PZ, NY), f32(8, NY), f32(8, NY),
        f32(*grid), f32(*grid), f32(*grid), f32(3, *grid), f32(3, *grid), f32(3, *grid),
        b16(NEAR, NY), b16(NEAR, NY), b16(FAR, NY), b16(FAR, NY),
        f32(3, 2 * ROWS, NY), f32(*halo), f32(8, NY),
        pltpu.SemaphoreType.DMA((16,)), pltpu.SemaphoreType.DMA((4,)),
        pltpu.SemaphoreType.DMA((144,)), pltpu.SemaphoreType.DMA((144,)),
    ]
    return pl.pallas_call(
        functools.partial(kernel, count_x),
        name="stokes",
        out_shape=[jax.ShapeDtypeStruct((3, *grid), F32), jax.ShapeDtypeStruct(grid, F32)],
        in_specs=[pl.BlockSpec(memory_space=pltpu.HBM)] * 12,
        out_specs=[any_spec] * 2,
        scratch_shapes=scratch,
        compiler_params=pltpu.CompilerParams(
            collective_id=0, has_side_effects=True, vmem_limit_bytes=62 << 20
        ),
    )(velocity, pressure, momentum, continuity, reaction, weight, mz_inverse, *consts)


def solution(mesh):
    return jax.shard_map(
        functools.partial(shards, mesh.shape["xy"]),
        mesh=mesh,
        in_specs=(
            P(None, "xy", "gz", None),
            P("xy", "gz", None),
            P(None, "xy", "gz", None),
            P("xy", "gz", None),
            P("xy", "gz", None),
            P("xy", None),
            P(),
        ),
        out_specs=(P(None, "xy", "gz", None), P("xy", "gz", None)),
        check_vma=False,
    )
```
